128 devices in a mesh: dp: 16 (over y, x), seq: 8 (over z, core).
Axes of the slice: x: 4, y: 4, z: 4, core: 2. Of those that a mesh axis runs over, the one named last changes fastest.
Arguments:
- queries: bfloat16 [16, 1024, 4096], P('dp', 'seq'), may hold values from -8 to 8
- grad_out: bfloat16 [16, 1024, 4096], P('dp', 'seq'), may hold values from -6 to 6
- kv_store: bfloat16 [16, 8, 640, 1024], P('dp', None, 'seq'), may hold values from -6 to 6
- tile_owner: int32 [16, 8], replicated, may hold values from 0 to 15, as said below
- tile_counts: int32 [16, 3], replicated, may hold values from 1 to 4, 8 in all within a row
- span_image: int32 [16, 8], replicated, may hold values from 0 to 2
Outputs:
- attn_out: bfloat16 [16, 1024, 4096], P('dp', 'seq')
- grad_q: bfloat16 [16, 1024, 4096], P('dp', 'seq')
- grad_kv: bfloat16 [16, 8, 640, 1024], P('dp', None, 'seq')
The draws below stay inside these ranges and needn't reach their ends.
Inputs may be any that keep to these rules, and one draw needn't show every extreme that they name: tile_owner[g, j] = (g + c_j) mod 16, one offset c_j for each slot j, the 8 offsets all different. `tile_counts`: the counts of one sample sum to 8.
All inputs are finite; a program needn't handle non-finite values.
Results may differ from the reference program's by a relative error of at most 0.012.
Values may be sent and summed in bfloat16 or wider, within the bound.
No kernel may reach another device: no remote copies, remote signals or barrier semaphores. Data moves between devices by JAX's collectives and lax.ppermute only.
A program may use at most 128 MiB of HBM per device.

```python
import math
import jax
import jax.numpy as jnp
import numpy as np
from jax import lax

HD = 128
HQ = 32
KVH = 4
GROUP = 8
TT = 640
TPS = 8
IMGS = 3
MAXT = 4
TOK_DEV = 128
SEQLEN = 1024
N_DP = 16
N_SEQ = 8


def draw_queries(key, part):
    key = jax.random.fold_in(key, 3)
    first = jax.random.fold_in(key, 0)
    shape = (N_DP, TOK_DEV * N_SEQ, HQ * HD)
    values = jnp.clip(jax.random.normal(first, shape, jnp.float32), -6.0, 6.0)
    return values.astype(jnp.bfloat16)


def draw_kv_store(key, part):
    key = jax.random.fold_in(key, 7)
    first = jax.random.fold_in(key, 0)
    shape = (N_DP, TPS, TT, 2 * KVH * HD)
    values = jnp.clip(jax.random.normal(first, shape, jnp.float32), -6.0, 6.0)
    return values.astype(jnp.bfloat16)


def draw_tile_owner(key, part):
    key = jax.random.fold_in(key, 5)
    offsets = jax.random.permutation(key, N_DP)[:TPS].astype(jnp.int32)
    samples = jnp.arange(N_DP, dtype=jnp.int32)[:, None]
    return ((samples + offsets[None, :]) % N_DP).astype(jnp.int32)


def set_ends(values, rng, smallest, high):
    longest = values.shape.index(max(values.shape))
    spots = []
    for shift in (0, 1):
        where = [jax.random.randint(jax.random.fold_in(rng, axis), (), 0, length) for axis, length in enumerate(values.shape)]
        where[longest] = (where[longest] + shift) % values.shape[longest]
        spots.append(tuple(where))
    return values.at[spots[0]].set(smallest).at[spots[1]].set(high)


def steps_of(stream_key, extent, pieces, low, largest):
    loudness, own = 1.0, jax.random.fold_in(stream_key, 6)
    for position, blocks in pieces:
        steps = jnp.exp(jax.random.uniform(jax.random.fold_in(own, position), (blocks,), jnp.float32, low / len(pieces), largest / len(pieces)))
        loudness = loudness * jnp.repeat(steps, extent[position] // blocks).reshape([-1 if axis == position else 1 for axis in range(len(extent))])
    return loudness


def profile(number_of, total, limit, slope):
    portions = [(1 << 20) // math.isqrt(rank ** slope) + 1 for rank in range(2, number_of + 1)]
    rest, holding = total - limit - (number_of - 1), [1] * (number_of - 1)
    while rest > 0:
        free = [i for i in range(number_of - 1) if holding[i] < limit]
        pool, budget = sum([portions[i] for i in free]), rest
        for i in free:
            extra = min(limit - holding[i], max(1, budget * portions[i] // pool), rest)
            holding[i] = holding[i] + extra
            rest = rest - extra
    return np.array([limit] + holding)


def ragged_sizes(stream_key, count, total, most, skew):
    if count == 2:
        one = jax.random.randint(stream_key, (), max(1, total - most), min(most, total - 1) + 1)
        return jnp.stack([one, total - one])
    sizes = jnp.asarray(profile(count, total, most, skew), jnp.int32)
    couples = (count - 1) // 2
    donor, taker = sizes[1:1 + 2 * couples:2], sizes[2:2 + 2 * couples:2]
    margin = jnp.minimum(donor - 1, most - taker)
    shifted = jax.random.randint(jax.random.fold_in(stream_key, 1), (couples,), 0, 1 << 20) % (margin + 1)
    sizes = sizes.at[1:1 + 2 * couples:2].set(donor - shifted).at[2:2 + 2 * couples:2].set(taker + shifted)
    return sizes[jax.random.permutation(jax.random.fold_in(stream_key, 2), count)]


def normal_values(rng, shape, width, most, shards=(), kind=jnp.bfloat16):
    result = jax.random.normal(rng, shape, jnp.float32) * width
    if len(shards) > 0:
        result = steps_of(rng, shape, shards, -0.22, 0.18) * result
    return jnp.clip(result, min=-most, max=most).astype(kind)


def setup_inputs(seed: int = 0) -> dict:
    arg_keys = jax.random.split(jax.random.key(seed), 7)
    queries = draw_queries(jax.random.fold_in(arg_keys[6], 71), 0)
    grad_out = normal_values(arg_keys[1], (N_DP, SEQLEN, HQ * HD), 1.0, 6.0, ((0, 16), (1, 8)))
    kv_store = draw_kv_store(jax.random.fold_in(arg_keys[6], 71), 0)
    tile_owner = draw_tile_owner(jax.random.fold_in(arg_keys[6], 71), 0)
    tile_counts = jax.vmap(lambda own: ragged_sizes(own, IMGS, TPS, MAXT, 0))(jax.random.split(arg_keys[4], N_DP)).reshape((N_DP, IMGS)).astype(jnp.int32)
    span_image = set_ends(jax.random.randint(arg_keys[5], (N_DP, N_SEQ), 0, IMGS), jax.random.fold_in(arg_keys[5], 1), 0, IMGS - 1).astype(jnp.int32)
    return dict(queries=queries, grad_out=grad_out, kv_store=kv_store, tile_owner=tile_owner, tile_counts=tile_counts, span_image=span_image)


def head_pass(q_head, d_head, key_block, value_block, usable):
    scaling = HD ** -0.5
    scores = jnp.dot(q_head, key_block.T, preferred_element_type=jnp.float32) * scaling
    scores = jnp.where(usable[None, :], scores, -1e30)
    top = jnp.max(scores, axis=-1, keepdims=True)
    expo = jnp.exp(scores - top)
    probs = expo / jnp.sum(expo, axis=-1, keepdims=True)
    probs_low = probs.astype(jnp.bfloat16)
    output = jnp.dot(probs_low, value_block, preferred_element_type=jnp.float32).astype(jnp.bfloat16)
    grad_probs = jnp.dot(d_head, value_block.T, preferred_element_type=jnp.float32)
    row_dot = jnp.sum(d_head.astype(jnp.float32) * output.astype(jnp.float32), axis=-1, keepdims=True)
    grad_scores = (probs * (grad_probs - row_dot)).astype(jnp.bfloat16)
    grad_query = (jnp.dot(grad_scores, key_block, preferred_element_type=jnp.float32) * scaling).astype(jnp.bfloat16)
    grad_key = (jnp.dot(grad_scores.T, q_head, preferred_element_type=jnp.float32) * scaling).astype(jnp.bfloat16)
    grad_value = jnp.dot(probs_low.T, d_head, preferred_element_type=jnp.float32).astype(jnp.bfloat16)
    return output, grad_query, grad_key, grad_value


def span_pass(q_rows, d_rows, keys_vals, usable):
    count_tok = q_rows.shape[0]
    q_heads = q_rows.reshape(count_tok, KVH, GROUP, HD).transpose(1, 2, 0, 3).reshape(KVH, GROUP * count_tok, HD)
    d_heads = d_rows.reshape(count_tok, KVH, GROUP, HD).transpose(1, 2, 0, 3).reshape(KVH, GROUP * count_tok, HD)
    split_kv = keys_vals.reshape(keys_vals.shape[0], 2, KVH, HD)
    key_heads = split_kv[:, 0].transpose(1, 0, 2)
    value_heads = split_kv[:, 1].transpose(1, 0, 2)
    outputs, grad_qs, grad_ks, grad_vs = lax.map(
        lambda packed: head_pass(packed[0], packed[1], packed[2], packed[3], usable),
        (q_heads, d_heads, key_heads, value_heads))
    attn_rows = outputs.reshape(KVH, GROUP, count_tok, HD).transpose(2, 0, 1, 3).reshape(count_tok, HQ * HD)
    grad_rows = grad_qs.reshape(KVH, GROUP, count_tok, HD).transpose(2, 0, 1, 3).reshape(count_tok, HQ * HD)
    both = jnp.concatenate([grad_ks, grad_vs], axis=0)
    parts = both.transpose(1, 0, 2).reshape(keys_vals.shape[0], 2 * KVH * HD)
    return attn_rows, grad_rows, parts


def reference(queries, grad_out, kv_store, tile_owner, tile_counts, span_image):
    slot_index = jnp.arange(TPS, dtype=jnp.int32)
    sample_tiles = kv_store[tile_owner, slot_index[None, :]]
    starts = (jnp.cumsum(tile_counts, axis=1) - tile_counts).astype(jnp.int32)
    order = jnp.arange(MAXT, dtype=jnp.int32)

    def per_sample(packed):
        q_sample, d_sample, tiles_sample, start_row, count_row, image_row = packed
        q_blocks = q_sample.reshape(N_SEQ, TOK_DEV, HQ * HD)
        d_blocks = d_sample.reshape(N_SEQ, TOK_DEV, HQ * HD)
        first = start_row[image_row]
        number = count_row[image_row]
        tile_ids = jnp.minimum(first[:, None] + order[None, :], TPS - 1).astype(jnp.int32)
        present = order[None, :] < number[:, None]

        def per_block(block):
            q_block, d_block, id_block, present_block = block
            keys_vals = tiles_sample[id_block].reshape(MAXT * TT, 2 * KVH * HD)
            usable = jnp.repeat(present_block, TT)
            attn_rows, grad_rows, parts = span_pass(q_block, d_block, keys_vals, usable)
            return attn_rows, grad_rows, parts.reshape(MAXT, TT, 2 * KVH * HD)

        attn_all, grad_all, parts_all = lax.map(per_block, (q_blocks, d_blocks, tile_ids, present))
        pick = ((tile_ids[:, :, None] == slot_index[None, None, :]) & present[:, :, None]).astype(jnp.float32)
        totals = jnp.einsum("ctj,ctrk->jrk", pick, parts_all.astype(jnp.float32))
        return attn_all.reshape(SEQLEN, HQ * HD), grad_all.reshape(SEQLEN, HQ * HD), totals

    attn_out, grad_q, totals = lax.map(per_sample, (queries, grad_out, sample_tiles, starts, tile_counts, span_image))
    owner_pick = (tile_owner[None, :, :] == jnp.arange(N_DP, dtype=jnp.int32)[:, None, None]).astype(jnp.float32)
    grad_kv = jnp.einsum("ogj,gjrk->ojrk", owner_pick, totals).astype(jnp.bfloat16)
    return attn_out, grad_q, grad_kv
```

```python
import jax
import jax.numpy as jnp
from jax import lax
from jax.experimental import pallas as pl
from jax.experimental.pallas import tpu as pltpu
from jax.sharding import PartitionSpec as P

HD = 128
HQ = 32
KVH = 4
TT = 640
TPS = 8
IMGS = 3
MAXT = 4
TOK = 128
N_SEQ = 8
ROWS = TT // N_SEQ
QH = HQ // N_SEQ
QW = QH * HD
HALF = TPS // 2
SCALE = HD**-0.5
EXP_SCALE = SCALE * 1.4426950408889634
BF = jnp.bfloat16
F32 = jnp.float32


def pick_rows(table, source, count):
    def body(_, s, o):
        o[...] = s[...]

    block = (1,) + source.shape[1:]
    zeros = (0,) * (source.ndim - 1)
    return pl.pallas_call(
        body,
        out_shape=jax.ShapeDtypeStruct((count,) + source.shape[1:], source.dtype),
        grid_spec=pltpu.PrefetchScalarGridSpec(
            num_scalar_prefetch=1,
            grid=(count,),
            in_specs=[pl.BlockSpec(block, lambda i, t: (t[i],) + zeros)],
            out_specs=pl.BlockSpec(block, lambda i, t: (i,) + zeros),
        ),
    )(table, source)


def tiles_by_head(table, arrived):
    def body(_, s, o):
        for h in range(KVH):
            o[h, 0, 0, :, :HD] = s[0, :, h * HD : (h + 1) * HD]
            o[h, 0, 0, :, HD:] = s[0, :, (KVH + h) * HD : (KVH + h + 1) * HD]

    return pl.pallas_call(
        body,
        out_shape=jax.ShapeDtypeStruct((KVH, 2, HALF, ROWS, 2 * HD), BF),
        grid_spec=pltpu.PrefetchScalarGridSpec(
            num_scalar_prefetch=1,
            grid=(TPS,),
            in_specs=[pl.BlockSpec((1, ROWS, 2 * KVH * HD), lambda j, t: (t[j], 0, 0))],
            out_specs=pl.BlockSpec(
                (KVH, 1, 1, ROWS, 2 * HD), lambda j, t: (0, j // HALF, j % HALF, 0, 0)
            ),
        ),
    )(table, arrived)


def tiles_from_heads(table, heads):
    def body(_, s, o):
        for h in range(KVH):
            o[0, :, h * HD : (h + 1) * HD] = s[h, 0, 0, :, :HD]
            o[0, :, (KVH + h) * HD : (KVH + h + 1) * HD] = s[h, 0, 0, :, HD:]

    count = table.shape[0]
    return pl.pallas_call(
        body,
        out_shape=jax.ShapeDtypeStruct((count, ROWS, 2 * KVH * HD), BF),
        grid_spec=pltpu.PrefetchScalarGridSpec(
            num_scalar_prefetch=1,
            grid=(count,),
            in_specs=[
                pl.BlockSpec(
                    (KVH, 1, 1, ROWS, 2 * HD), lambda o, t: (0, t[o] // HALF, t[o] % HALF, 0, 0)
                )
            ],
            out_specs=pl.BlockSpec((1, ROWS, 2 * KVH * HD), lambda o, t: (o, 0, 0)),
        ),
    )(table, heads)


def split_heads(left, right):
    def body(a, b, o):
        o[0, :, :QW] = a[...]
        o[0, :, QW:] = b[...]

    spec = pl.BlockSpec((TOK, QW), lambda i: (0, i))
    return pl.pallas_call(
        body,
        out_shape=jax.ShapeDtypeStruct((N_SEQ, TOK, 2 * QW), BF),
        grid=(N_SEQ,),
        in_specs=[spec, spec],
        out_specs=pl.BlockSpec((1, TOK, 2 * QW), lambda i: (i, 0, 0)),
    )(left, right)


def join_heads(both):
    def body(s, a, b):
        a[...] = s[0, :, :QW]
        b[...] = s[0, :, QW:]

    spec = pl.BlockSpec((TOK, QW), lambda i: (0, i))
    shape = jax.ShapeDtypeStruct((TOK, HQ * HD), BF)
    return pl.pallas_call(
        body,
        out_shape=(shape, shape),
        grid=(N_SEQ,),
        in_specs=[pl.BlockSpec((1, TOK, 2 * QW), lambda i: (i, 0, 0))],
        out_specs=(spec, spec),
    )(both)


def attention_body(
    info, qd, kv_mine, kv_other, out, grad_mine, grad_other,
    k_s, v_s, kt_s, vt_s, dkt_s, dvt_s, s_s, q_s, d_s, qt_s, dt_s,
    m_s, l_s, o_s, r_s, ds_s, pb_s,
):
    b = pl.program_id(0)
    core = info[2, 0]
    lanes = [slice(i * HD, (i + 1) * HD) for i in range(TT // HD)]
    heads = [slice(h * TOK, (h + 1) * TOK) for h in range(QH)]

    @pl.when(b == 0)
    def _():
        for source, base in ((kv_mine, core * HALF), (kv_other, (1 - core) * HALF)):

            @pl.loop(0, HALF)
            def _(i):
                j = base + i
                for s in range(N_SEQ):
                    k_s[j, s * ROWS : (s + 1) * ROWS, :] = source[s, i, :, :HD]
                    v_s[j, s * ROWS : (s + 1) * ROWS, :] = source[s, i, :, HD:]
                kt_s[j] = k_s[j].T
                vt_s[j] = v_s[j].T
                dkt_s[j] = jnp.zeros((HD, TT), F32)
                dvt_s[j] = jnp.zeros((HD, TT), F32)

    for h, rows in enumerate(heads):
        q_s[rows, :] = qd[0, :, h * HD : (h + 1) * HD]
        d_s[rows, :] = qd[0, :, QW + h * HD : QW + (h + 1) * HD]
    qt_s[...] = q_s[...].T
    dt_s[...] = d_s[...].T
    first, number = info[0, b], info[1, b]
    m_s[...] = jnp.full(m_s.shape, -jnp.inf, F32)
    l_s[...] = jnp.zeros_like(l_s)
    o_s[...] = jnp.zeros_like(o_s)

    @pl.loop(0, number)
    def _(t):
        j = first + t
        for rows in heads:
            s = jnp.dot(q_s[rows, :], kt_s[j], preferred_element_type=F32)
            s_s[t, rows, :] = s
            top = m_s[rows, :]
            for part in lanes:
                top = jnp.maximum(top, s[:, part])
            m_s[rows, :] = top

    for rows in heads:
        m_s[rows, :] = jnp.broadcast_to(jnp.max(m_s[rows, :], axis=1, keepdims=True), (TOK, HD))

    @pl.loop(0, number)
    def _(t):
        j = first + t
        for rows in heads:
            top = m_s[rows, :]
            total = l_s[rows, :]
            low = []
            for part in lanes:
                e = jnp.exp2((s_s[t, rows, part] - top) * EXP_SCALE)
                s_s[t, rows, part] = e
                total = total + e
                low.append(e.astype(BF))
            l_s[rows, :] = total
            o_s[rows, :] += jnp.dot(
                jnp.concatenate(low, axis=1), v_s[j], preferred_element_type=F32
            )

    for h, rows in enumerate(heads):
        inverse = 1.0 / jnp.sum(l_s[rows, :], axis=1, keepdims=True)
        inverse = jnp.broadcast_to(inverse, (TOK, HD))
        l_s[rows, :] = inverse
        attn = (o_s[rows, :] * inverse).astype(BF)
        out[0, :, h * HD : (h + 1) * HD] = attn
        dot = jnp.sum(d_s[rows, :].astype(F32) * attn.astype(F32), axis=1, keepdims=True)
        r_s[rows, :] = jnp.broadcast_to(dot, (TOK, HD))
    o_s[...] = jnp.zeros_like(o_s)

    @pl.loop(0, number)
    def _(t):
        j = first + t
        for rows in heads:
            dp = jnp.dot(d_s[rows, :], vt_s[j], preferred_element_type=F32)
            inverse = l_s[rows, :]
            dot = r_s[rows, :]
            low = []
            for part in lanes:
                p = s_s[t, rows, part] * inverse
                pb_s[rows, part] = p.astype(BF)
                low.append((p * (dp[:, part] - dot)).astype(BF))
            ds = jnp.concatenate(low, axis=1)
            ds_s[rows, :] = ds
            o_s[rows, :] += jnp.dot(ds, k_s[j], preferred_element_type=F32)
        dkt_s[j] += jnp.dot(qt_s[...], ds_s[...], preferred_element_type=F32)
        dvt_s[j] += jnp.dot(dt_s[...], pb_s[...], preferred_element_type=F32)

    for h, rows in enumerate(heads):
        out[0, :, QW + h * HD : QW + (h + 1) * HD] = (o_s[rows, :] * SCALE).astype(BF)

    @pl.when(b == N_SEQ - 1)
    def _():
        for target, base in ((grad_mine, core * HALF), (grad_other, (1 - core) * HALF)):

            @pl.loop(0, HALF)
            def _(i):
                j = base + i
                dk = (dkt_s[j] * SCALE).T.astype(target.dtype)
                dv = dvt_s[j].T.astype(target.dtype)
                for s in range(N_SEQ):
                    target[s, i, :, :HD] = dk[s * ROWS : (s + 1) * ROWS, :]
                    target[s, i, :, HD:] = dv[s * ROWS : (s + 1) * ROWS, :]


def attention(info, qd, kv_mine, kv_other):
    part = (N_SEQ, HALF, ROWS, 2 * HD)
    whole = pl.BlockSpec(part, lambda b, t: (0, 0, 0, 0), pipeline_mode=pl.Buffered(1))
    block = pl.BlockSpec((1, TOK, 2 * QW), lambda b, t: (b, 0, 0))
    rows = QH * TOK
    return pl.pallas_call(
        attention_body,
        out_shape=(
            jax.ShapeDtypeStruct((N_SEQ, TOK, 2 * QW), BF),
            jax.ShapeDtypeStruct(part, F32),
            jax.ShapeDtypeStruct(part, BF),
        ),
        grid_spec=pltpu.PrefetchScalarGridSpec(
            num_scalar_prefetch=1,
            grid=(N_SEQ,),
            in_specs=[block, whole, whole],
            out_specs=(
                block,
                pl.BlockSpec(part, lambda b, t: (0, 0, 0, 0)),
                pl.BlockSpec(part, lambda b, t: (0, 0, 0, 0)),
            ),
            scratch_shapes=[
                pltpu.VMEM((TPS, TT, HD), BF),
                pltpu.VMEM((TPS, TT, HD), BF),
                pltpu.VMEM((TPS, HD, TT), BF),
                pltpu.VMEM((TPS, HD, TT), BF),
                pltpu.VMEM((TPS, HD, TT), F32),
                pltpu.VMEM((TPS, HD, TT), F32),
                pltpu.VMEM((MAXT, rows, TT), F32),
                pltpu.VMEM((rows, HD), BF),
                pltpu.VMEM((rows, HD), BF),
                pltpu.VMEM((HD, rows), BF),
                pltpu.VMEM((HD, rows), BF),
                pltpu.VMEM((rows, HD), F32),
                pltpu.VMEM((rows, HD), F32),
                pltpu.VMEM((rows, HD), F32),
                pltpu.VMEM((rows, HD), F32),
                pltpu.VMEM((rows, TT), BF),
                pltpu.VMEM((rows, TT), BF),
            ],
        ),
        compiler_params=pltpu.CompilerParams(vmem_limit_bytes=56 * 2**20),
        cost_estimate=pl.CostEstimate(
            flops=12 * rows * N_SEQ * 3 * TT * HD, bytes_accessed=12 * 2**20, transcendentals=0
        ),
    )(info, qd, kv_mine, kv_other)


def shards(queries, grad_out, kv_store, tile_owner, tile_counts, span_image):
    my_group = lax.axis_index("dp")
    my_seq = lax.axis_index("seq")
    slots = jnp.arange(TPS, dtype=jnp.int32)

    mine = (tile_owner == my_group).astype(jnp.int32)
    slot_for = jnp.sum(mine * slots[None, :], axis=1)
    group_of = jnp.sum(
        mine * jnp.arange(tile_owner.shape[0], dtype=jnp.int32)[:, None], axis=0
    )
    owner = lax.dynamic_index_in_dim(tile_owner, my_group, 0, keepdims=False)
    groups = jnp.arange(tile_owner.shape[0], dtype=jnp.int32)
    slot_from = jnp.sum((owner[None, :] == groups[:, None]) * slots[None, :], axis=1).astype(
        jnp.int32
    )
    counts = lax.dynamic_index_in_dim(tile_counts, my_group, 0, keepdims=False)
    starts = jnp.cumsum(counts) - counts
    images = lax.dynamic_index_in_dim(span_image, my_group, 0, keepdims=False)
    image_pick = images[:, None] == jnp.arange(IMGS, dtype=jnp.int32)[None, :]
    first = jnp.sum(jnp.where(image_pick, starts[None, :], 0), axis=1)
    number = jnp.sum(jnp.where(image_pick, counts[None, :], 0), axis=1)
    core = jnp.broadcast_to(my_seq % 2, (N_SEQ,))
    info = jnp.stack([first, number, core]).astype(jnp.int32)

    qd = split_heads(queries[0], grad_out[0])
    qd = lax.all_to_all(qd, "seq", split_axis=0, concat_axis=0, tiled=True)

    outgoing = pick_rows(slot_for, kv_store[0], groups.shape[0])
    arrived = lax.all_to_all(outgoing, "dp", split_axis=0, concat_axis=0, tiled=True)
    by_head = tiles_by_head(owner, arrived).reshape(N_SEQ, HALF, ROWS, 2 * HD)
    kv_mine = lax.all_to_all(by_head, "seq", split_axis=0, concat_axis=0, tiled=True)
    pair = [(i, i ^ 1) for i in range(N_SEQ)]
    kv_other = lax.ppermute(kv_mine, "seq", pair)

    out, grad_mine, grad_other = attention(info, qd, kv_mine, kv_other)

    grad_sent = lax.ppermute(grad_other, "seq", pair)
    summed = (grad_mine + grad_sent.astype(F32)).astype(BF)
    back = lax.all_to_all(summed, "seq", split_axis=0, concat_axis=0, tiled=True)
    homeward = tiles_from_heads(slot_from, back.reshape(KVH, 2, HALF, ROWS, 2 * HD))
    received = lax.all_to_all(homeward, "dp", split_axis=0, concat_axis=0, tiled=True)
    grad_kv = pick_rows(group_of, received, TPS)

    out = lax.all_to_all(out, "seq", split_axis=0, concat_axis=0, tiled=True)
    attn_rows, grad_rows = join_heads(out)
    return (attn_rows[None], grad_rows[None], grad_kv[None])


def solution(mesh):
    placed = (P("dp", "seq", None), P("dp", "seq", None), P("dp", None, "seq", None), P(), P(), P())
    return jax.shard_map(
        shards,
        mesh=mesh,
        in_specs=placed,
        out_specs=(P("dp", "seq", None), P("dp", "seq", None), P("dp", None, "seq", None)),
        check_vma=False,
    )
```

```python
import jax
import jax.numpy as jnp
from jax import lax
from jax.experimental import pallas as pl
from jax.experimental.pallas import tpu as pltpu
from jax.sharding import PartitionSpec as P

HD = 128
HQ = 32
KVH = 4
GROUP = 8
TT = 640
TPS = 8
IMGS = 3
MAXT = 4
TOK = 128
N_SEQ = 8
CHIPS = 4
ROWS = TT // N_SEQ
KW = KVH * HD
QW = GROUP * HD
LINES = GROUP * TOK
SCALE = HD**-0.5
PIECE = (TPS, ROWS, HD)
PIECES = (TPS, CHIPS, ROWS, HD)
EXP_SCALE = SCALE * 1.4426950408889634
BF = jnp.bfloat16
F32 = jnp.float32


def run_copies(pairs):
    for (source, where), (target, there) in pairs:
        target[there] = source[where]


def whole(shape):
    zeros = (0,) * len(shape)
    return pl.BlockSpec(shape, lambda i, t: zeros)


def copier(body, shapes, table, *arrays, after=()):
    return pl.pallas_call(
        body,
        out_shape=shapes,
        grid_spec=pltpu.PrefetchScalarGridSpec(
            num_scalar_prefetch=1,
            grid=(1,),
            in_specs=[whole(a.shape) for a in arrays]
            + [pl.BlockSpec(memory_space=pl.ANY)] * len(after),
            out_specs=jax.tree.map(lambda a: whole(a.shape), shapes),
        ),
        compiler_params=pltpu.CompilerParams(vmem_limit_bytes=32 * 2**20),
    )(table, *arrays, *after)


def struct(*shape):
    return jax.ShapeDtypeStruct(shape, BF)


def column(index, width):
    return pl.ds(pl.multiple_of(index * width, width), width)


def outgoing_heads(peers, store, part, *text):
    def body(t, s, *rest):
        outs = rest[len(text) :]
        for k in range(CHIPS):
            outs[k][...] = s[:, :, column(t[k], HD)]
        for i in range(len(text)):
            for k in range(1, CHIPS):
                outs[CHIPS + 3 * i + k - 1][...] = rest[i][:, column(t[k], QW)]

    shapes = (struct(*PIECE),) * CHIPS + (struct(TOK, QW),) * (3 * len(text))
    return pl.pallas_call(
        body,
        out_shape=shapes,
        grid_spec=pltpu.PrefetchScalarGridSpec(
            num_scalar_prefetch=1,
            grid=(1,),
            in_specs=[pl.BlockSpec((TPS, ROWS, KW), lambda i, t: (0, 0, part))]
            + [whole(x.shape) for x in text],
            out_specs=jax.tree.map(lambda a: whole(a.shape), shapes),
        ),
        compiler_params=pltpu.CompilerParams(vmem_limit_bytes=32 * 2**20),
    )(peers, store, *text)


def fence(x, *after):
    def body(*refs):
        pass

    return pl.pallas_call(
        body,
        out_shape=jax.ShapeDtypeStruct(x.shape, x.dtype),
        in_specs=[pl.BlockSpec(memory_space=pl.ANY)] * (1 + len(after)),
        out_specs=pl.BlockSpec(memory_space=pl.ANY),
        input_output_aliases={0: 0},
    )(x, *after)


def outgoing_pieces(group_of, pieces, *after):
    def body(t, *rest):
        for j in range(TPS):
            for k in range(CHIPS):
                rest[-1][t[j], k] = rest[k][j]

    return copier(body, struct(16, *PIECES[1:]), group_of, *pieces, after=after)


def chosen(table, arrived, *after):
    def body(t, s, *rest):
        for j in range(TPS):
            rest[-1][j] = s[t[j]]

    return copier(body, struct(*PIECES), table, arrived, after=after)


def outgoing_sums(owner, own, other):
    def body(t, a, b, *rest):
        for j in range(TPS):
            rest[-1][t[j]] = (a[j] + b[j].astype(F32)).astype(BF)

    return copier(body, struct(16, *PIECES[1:]), owner, own, other)


def chosen_pieces(group_of, arrived):
    def body(t, s, *outs):
        for j in range(TPS):
            for k in range(CHIPS):
                outs[k][j] = s[t[j], k]

    return copier(body, (struct(*PIECE),) * CHIPS, group_of, arrived)


def stored_tiles(peers, keys, values):
    def body(t, *rest):
        for part in range(2):
            for k in range(CHIPS):
                where = column(t[k] + part * KVH, HD)
                rest[-1][:, :, where] = rest[part * CHIPS + k][...]

    return copier(body, struct(TPS, ROWS, 2 * KW), peers, *keys, *values)


def text_rows(peers, chunks):
    def body(t, *rest):
        for k in range(CHIPS):
            rest[CHIPS][:, column(t[k], QW)] = rest[k][...]

    return copier(body, struct(TOK, HQ * HD), peers, *chunks)


LANES = [slice(i * HD, (i + 1) * HD) for i in range(TT // HD)]
HEADS = [slice(h * TOK, (h + 1) * TOK) for h in range(GROUP)]
CH_S, CH_O, CH_D = 256, 512, 512


def cuts(size):
    return [slice(i, i + size) for i in range(0, LINES, size)]


def wide(column, rows):
    return jnp.broadcast_to(column, (rows, HD))


def fill_tiles(core, target, mine, other):
    for k in range(CHIPS):
        here = pl.multiple_of(core * (TT // 2) + k * ROWS, 16)
        there = pl.multiple_of((1 - core) * (TT // 2) + k * ROWS, 16)

        @pl.loop(0, TPS)
        def _(j):
            target[j, pl.ds(here, ROWS), :] = mine[j, k]
            target[j, pl.ds(there, ROWS), :] = other[j, k]


def split_tiles(core, total, scale, mine, other):
    @pl.loop(0, TPS)
    def _(j):
        rows = (total[j] * scale).T
        halves = [rows[: TT // 2].reshape(CHIPS, ROWS, HD), rows[TT // 2 :].reshape(CHIPS, ROWS, HD)]
        for p in range(2):

            @pl.when(core == p)
            def _():
                mine[j] = halves[p]
                other[j] = halves[1 - p].astype(BF)


def load_text(b, target, chunks):
    for k, chunk in enumerate(chunks):

        @pl.when(b == k)
        def _():
            for h, rows in enumerate(HEADS):
                target[rows, :] = chunk[:, h * HD : (h + 1) * HD]


def store_text(b, chunks, value):
    for k, chunk in enumerate(chunks):

        @pl.when(b == k)
        def _():
            for h, rows in enumerate(HEADS):
                chunk[:, h * HD : (h + 1) * HD] = value(rows)


def weights_body(
    info, q0, q1, q2, q3, k_mine, k_other, e_out, w_out, k_s, kt_s, q_s, m_s, l_s, top_s, sum_s
):
    b = pl.program_id(0)
    first, number = info[0, b], info[1, b]

    @pl.when(b == 0)
    def _():
        fill_tiles(info[2, 1], k_s, k_mine, k_other)

        @pl.loop(0, TPS)
        def _(j):
            kt_s[j] = k_s[j].T

    load_text(b, q_s, (q0, q1, q2, q3))
    top_s[...] = jnp.full(top_s.shape, -jnp.inf, F32)
    sum_s[...] = jnp.zeros_like(sum_s)
    w_out[...] = jnp.zeros_like(w_out)

    @pl.loop(0, number)
    def _(t):
        j = first + t
        for rows in cuts(CH_S):
            s = jnp.dot(q_s[rows, :], kt_s[j], preferred_element_type=F32)
            top = s[:, LANES[0]]
            for part in LANES[1:]:
                top = jnp.maximum(top, s[:, part])
            top = wide(jnp.max(top, axis=1, keepdims=True), CH_S)
            m_s[t, rows, :] = top
            top_s[rows, :] = jnp.maximum(top_s[rows, :], top)
            top = top * EXP_SCALE
            total = None
            for part in LANES:
                e = jnp.exp2(s[:, part] * EXP_SCALE - top)
                e_out[0, t, rows, part] = e.astype(BF)
                total = e if total is None else total + e
            l_s[t, rows, :] = total

    @pl.loop(0, number)
    def _(t):
        f = jnp.exp2((m_s[t] - top_s[...]) * EXP_SCALE)
        m_s[t] = f
        sum_s[...] += f * l_s[t]

    for rows in HEADS:
        total = jnp.sum(sum_s[rows, :], axis=1, keepdims=True)
        sum_s[rows, :] = wide(1.0 / total, TOK)

    @pl.loop(0, number)
    def _(t):
        lane = lax.broadcasted_iota(jnp.int32, W_SHAPE, 1)
        w_out[0] = jnp.where(lane == t, m_s[t] * sum_s[...], w_out[0])


def outputs_body(
    info, g0, g1, g2, g3, e, w, v_mine, v_other, o0, o1, o2, o3, d_out, mine, other,
    v_s, dvt_s, d_s, acc_s,
):
    b = pl.program_id(0)
    core = info[2, 1]
    first, number = info[0, b], info[1, b]

    @pl.when(b == 0)
    def _():
        fill_tiles(core, v_s, v_mine, v_other)

        @pl.loop(0, TPS)
        def _(j):
            dvt_s[j] = jnp.zeros((HD, TT), F32)

    load_text(b, d_s, (g0, g1, g2, g3))
    acc_s[...] = jnp.zeros_like(acc_s)

    @pl.loop(0, number)
    def _(t):
        j = first + t
        lane = lax.broadcasted_iota(jnp.int32, (CH_O, HD), 1)
        for rows in cuts(CH_O):
            weight = jnp.sum(jnp.where(lane == t, w[0, rows, :], 0.0), axis=1, keepdims=True)
            acc_s[rows, :] += weight * jnp.dot(e[0, t, rows, :], v_s[j], preferred_element_type=F32)
            d_out[0, t, rows, :] = (d_s[rows, :].astype(F32) * weight).astype(BF)
        dvt_s[j] += jnp.dot(d_out[0, t].T, e[0, t], preferred_element_type=F32)

    store_text(b, (o0, o1, o2, o3), lambda rows: acc_s[rows, :].astype(BF))

    @pl.when(b == CHIPS - 1)
    def _():
        split_tiles(core, dvt_s, 1.0, mine, other)


def grads_body(
    info, q0, q1, q2, q3, e, d, a0, a1, a2, a3, k_mine, k_other, v_mine, v_other,
    o0, o1, o2, o3, mine, other,
    k_s, vt_s, dkt_s, q_s, acc_s, a_s, ds_s,
):
    b = pl.program_id(0)
    core = info[2, 1]
    first, number = info[0, b], info[1, b]

    @pl.when(b == 0)
    def _():
        fill_tiles(core, k_s, v_mine, v_other)

        @pl.loop(0, TPS)
        def _(j):
            vt_s[j] = k_s[j].T
            dkt_s[j] = jnp.zeros((HD, TT), F32)

        fill_tiles(core, k_s, k_mine, k_other)

    load_text(b, q_s, (q0, q1, q2, q3))
    load_text(b, a_s, (a0, a1, a2, a3))
    acc_s[...] = jnp.zeros_like(acc_s)

    @pl.loop(0, number)
    def _(t):
        j = first + t
        for rows in cuts(CH_D):
            dp = jnp.dot(d[0, t, rows, :], vt_s[j], preferred_element_type=F32)
            dot = jnp.sum(
                d[0, t, rows, :].astype(F32) * a_s[rows, :].astype(F32), axis=1, keepdims=True
            )
            ds = (e[0, t, rows, :].astype(F32) * (dp - dot)).astype(BF)
            ds_s[rows, :] = ds
            acc_s[rows, :] += jnp.dot(ds, k_s[j], preferred_element_type=F32)
        dkt_s[j] += jnp.dot(q_s[...].T, ds_s[...], preferred_element_type=F32)

    store_text(b, (o0, o1, o2, o3), lambda rows: (acc_s[rows, :] * SCALE).astype(BF))

    @pl.when(b == CHIPS - 1)
    def _():
        split_tiles(core, dkt_s, SCALE, mine, other)


def fixed(shape):
    zeros = (0,) * len(shape)
    return pl.BlockSpec(shape, lambda b, t: zeros, pipeline_mode=pl.Buffered(1))


def kept(shape):
    zeros = (0,) * len(shape)
    return pl.BlockSpec(shape, lambda b, t: zeros)


def by_block(*shape):
    zeros = (0,) * len(shape)
    return pl.BlockSpec((1,) + shape, lambda b, t: (b,) + zeros)


OWN_TEXT = pl.BlockSpec((TOK, QW), lambda b, t: (0, t[2, 0]), pipeline_mode=pl.Buffered(1))
E_SHAPE = (MAXT, LINES, TT)
D_SHAPE = (MAXT, LINES, HD)
W_SHAPE = (LINES, HD)


def attention_call(body, matmuls, out_shape, in_specs, out_specs, scratch_shapes):
    return pl.pallas_call(
        body,
        out_shape=out_shape,
        grid_spec=pltpu.PrefetchScalarGridSpec(
            num_scalar_prefetch=1,
            grid=(CHIPS,),
            in_specs=in_specs,
            out_specs=out_specs,
            scratch_shapes=scratch_shapes,
        ),
        compiler_params=pltpu.CompilerParams(vmem_limit_bytes=56 * 2**20),
        cost_estimate=pl.CostEstimate(
            flops=20 * matmuls * LINES * CHIPS * 3 * TT * HD,
            bytes_accessed=30 * 2**20,
            transcendentals=0,
        ),
    )


TEXT = [OWN_TEXT] + [fixed((TOK, QW))] * 3
TEXT_OUT = (struct(TOK, QW),) * 4
TEXT_KEPT = (kept((TOK, QW)),) * 4
TILES = [fixed(PIECES)] * 2
TILES_OUT = (jax.ShapeDtypeStruct(PIECES, F32), struct(*PIECES))
TILES_KEPT = (kept(PIECES),) * 2
TILE_ROWS, TILE_COLUMNS = (TPS, TT, HD), (TPS, HD, TT)


def weights(info, queries, tiles):
    return attention_call(
        weights_body,
        2,
        (struct(CHIPS, *E_SHAPE), jax.ShapeDtypeStruct((CHIPS,) + W_SHAPE, F32)),
        TEXT + TILES,
        (by_block(*E_SHAPE), by_block(*W_SHAPE)),
        [
            pltpu.VMEM(TILE_ROWS, BF),
            pltpu.VMEM(TILE_COLUMNS, BF),
            pltpu.VMEM((LINES, HD), BF),
            pltpu.VMEM((MAXT, LINES, HD), F32),
            pltpu.VMEM((MAXT, LINES, HD), F32),
            pltpu.VMEM((LINES, HD), F32),
            pltpu.VMEM((LINES, HD), F32),
        ],
    )(info, *queries, *tiles)


def outputs(info, grads, e, w, tiles):
    return attention_call(
        outputs_body,
        2,
        TEXT_OUT + (struct(CHIPS, *D_SHAPE),) + TILES_OUT,
        TEXT + [by_block(*E_SHAPE), by_block(*W_SHAPE)] + TILES,
        TEXT_KEPT + (by_block(*D_SHAPE),) + TILES_KEPT,
        [
            pltpu.VMEM(TILE_ROWS, BF),
            pltpu.VMEM(TILE_COLUMNS, F32),
            pltpu.VMEM((LINES, HD), BF),
            pltpu.VMEM((LINES, HD), F32),
        ],
    )(info, *grads, e, w, *tiles)


def gradients(info, queries, e, d, attn, keys, values):
    return attention_call(
        grads_body,
        3,
        TEXT_OUT + TILES_OUT,
        TEXT
        + [by_block(*E_SHAPE), by_block(*D_SHAPE)]
        + [fixed((TOK, QW))] * 4
        + TILES * 2,
        TEXT_KEPT + TILES_KEPT,
        [
            pltpu.VMEM(TILE_ROWS, BF),
            pltpu.VMEM(TILE_COLUMNS, BF),
            pltpu.VMEM(TILE_COLUMNS, F32),
            pltpu.VMEM((LINES, HD), BF),
            pltpu.VMEM((LINES, HD), F32),
            pltpu.VMEM((LINES, HD), BF),
            pltpu.VMEM((LINES, TT), BF),
        ],
    )(info, *queries, e, d, *attn, *keys, *values)


def swap(x, mask):
    return lax.ppermute(x, "seq", [(i, i ^ mask) for i in range(N_SEQ)])


def spread(chunks):
    return [chunks[0]] + [swap(chunks[k], 2 * k) for k in range(1, CHIPS)]


def shards(queries, grad_out, kv_store, tile_owner, tile_counts, span_image):
    my_group = lax.axis_index("dp")
    my_seq = lax.axis_index("seq")
    chip, core = my_seq // 2, my_seq % 2
    queries, grad_out, store = queries[0], grad_out[0], kv_store[0]

    groups = jnp.arange(tile_owner.shape[0], dtype=jnp.int32)
    group_of = jnp.sum(jnp.where(tile_owner == my_group, groups[:, None], 0), axis=0).astype(
        jnp.int32
    )
    owner = lax.dynamic_index_in_dim(tile_owner, my_group, 0, keepdims=False)
    peers = (chip ^ jnp.arange(CHIPS, dtype=jnp.int32)).astype(jnp.int32)
    counts = lax.dynamic_index_in_dim(tile_counts, my_group, 0, keepdims=False)
    starts = jnp.cumsum(counts) - counts
    images = lax.dynamic_index_in_dim(span_image, my_group, 0, keepdims=False)
    blocks = peers * 2 + core
    mine = jnp.sum(
        jnp.where(blocks[:, None] == jnp.arange(N_SEQ)[None, :], images[None, :], 0), axis=1
    )
    pick = mine[:, None] == jnp.arange(IMGS, dtype=jnp.int32)[None, :]
    first = jnp.sum(jnp.where(pick, starts[None, :], 0), axis=1)
    number = jnp.sum(jnp.where(pick, counts[None, :], 0), axis=1)
    place = jnp.stack([chip, core, chip, core])
    info = jnp.stack([first, number, place]).astype(jnp.int32)

    def exchange(x):
        return lax.all_to_all(x, "dp", split_axis=0, concat_axis=0, tiled=True)

    k_pieces = outgoing_heads(peers, store, 0)
    pieces = outgoing_heads(peers, store, 1, queries, grad_out)
    v_pieces, texts = pieces[:CHIPS], pieces[CHIPS:]
    q_text = spread([queries, *texts[:3]])
    g_text = spread([grad_out, *texts[3:]])
    keys = exchange(outgoing_pieces(group_of, spread(k_pieces), v_pieces[0]))
    values = outgoing_pieces(group_of, spread(v_pieces), info, *q_text[1:])
    keys = chosen(owner, keys, values)
    keys = keys, swap(keys, 1)
    e, w = weights(info, q_text, keys)
    values = chosen(owner, exchange(values), w, *g_text[1:])
    values = values, swap(values, 1)

    *attn, d, dv_mine, dv_other = outputs(info, g_text, e, w, values)
    attn_text = spread(attn)
    *grad_q, dk_mine, dk_other = gradients(info, q_text, e, d, attn, keys, values)
    dk_other = fence(dk_other, *attn_text[1:])

    def scatter(own, other):
        arrived = exchange(outgoing_sums(owner, own, swap(other, 1)))
        return spread(chosen_pieces(group_of, arrived))

    dv = scatter(dv_mine, dv_other)
    dk = scatter(dk_mine, dk_other)
    grad_kv = stored_tiles(peers, dk, dv)
    attn_rows = text_rows(peers, attn_text)
    grad_rows = text_rows(peers, spread(grad_q))
    return (attn_rows[None], grad_rows[None], grad_kv[None])


def solution(mesh):
    placed = (P("dp", "seq", None), P("dp", "seq", None), P("dp", None, "seq", None), P(), P(), P())
    return jax.shard_map(
        shards,
        mesh=mesh,
        in_specs=placed,
        out_specs=(P("dp", "seq", None), P("dp", "seq", None), P("dp", None, "seq", None)),
        check_vma=False,
    )
```

```python
import jax
import jax.numpy as jnp
from jax import lax
from jax.experimental import pallas as pl
from jax.experimental.pallas import tpu as pltpu
from jax.sharding import PartitionSpec as P

HD = 128
HQ = 32
KVH = 4
GROUP = 8
TT = 640
TPS = 8
IMGS = 3
MAXT = 4
TOK = 128
N_SEQ = 8
CHIPS = 4
ROWS = TT // N_SEQ
KW = KVH * HD
QW = GROUP * HD
LINES = GROUP * TOK
SCALE = HD**-0.5
PIECE = (TPS, ROWS, HD)
PIECES = (TPS, CHIPS, ROWS, HD)
EXP_SCALE = SCALE * 1.4426950408889634
LONG = 10**11
BF = jnp.bfloat16
F32 = jnp.float32


def run_copies(pairs):
    for (source, where), (target, there) in pairs:
        target[there] = source[where]


def whole(shape):
    zeros = (0,) * len(shape)
    return pl.BlockSpec(shape, lambda i, t: zeros)


def copier(body, shapes, table, *arrays, after=(), flops=0):
    return pl.pallas_call(
        body,
        out_shape=shapes,
        grid_spec=pltpu.PrefetchScalarGridSpec(
            num_scalar_prefetch=1,
            grid=(1,),
            in_specs=[whole(a.shape) for a in arrays]
            + [pl.BlockSpec(memory_space=pl.ANY)] * len(after),
            out_specs=jax.tree.map(lambda a: whole(a.shape), shapes),
        ),
        compiler_params=pltpu.CompilerParams(vmem_limit_bytes=32 * 2**20),
        cost_estimate=pl.CostEstimate(flops=flops, bytes_accessed=2**22, transcendentals=0),
    )(table, *arrays, *after)


def struct(*shape):
    return jax.ShapeDtypeStruct(shape, BF)


def column(index, width):
    return pl.ds(pl.multiple_of(index * width, width), width)


def outgoing_heads(peers, store, part, *text):
    def body(t, s, *rest):
        outs = rest[len(text) :]
        for k in range(CHIPS):
            outs[k][...] = s[:, :, column(t[k], HD)]
        for i in range(len(text)):
            for k in range(1, CHIPS):
                outs[CHIPS + 3 * i + k - 1][...] = rest[i][:, column(t[k], QW)]

    shapes = (struct(*PIECE),) * CHIPS + (struct(TOK, QW),) * (3 * len(text))
    return pl.pallas_call(
        body,
        out_shape=shapes,
        grid_spec=pltpu.PrefetchScalarGridSpec(
            num_scalar_prefetch=1,
            grid=(1,),
            in_specs=[pl.BlockSpec((TPS, ROWS, KW), lambda i, t: (0, 0, part))]
            + [whole(x.shape) for x in text],
            out_specs=jax.tree.map(lambda a: whole(a.shape), shapes),
        ),
        compiler_params=pltpu.CompilerParams(vmem_limit_bytes=32 * 2**20),
    )(peers, store, *text)


def fence(x, *after):
    def body(*refs):
        pass

    return pl.pallas_call(
        body,
        out_shape=jax.ShapeDtypeStruct(x.shape, x.dtype),
        in_specs=[pl.BlockSpec(memory_space=pl.ANY)] * (1 + len(after)),
        out_specs=pl.BlockSpec(memory_space=pl.ANY),
        input_output_aliases={0: 0},
    )(x, *after)


def outgoing_pieces(group_of, pieces, *after):
    def body(t, *rest):
        for j in range(TPS):
            for k in range(CHIPS):
                rest[-1][t[j], k] = rest[k][j]

    return copier(body, struct(16, *PIECES[1:]), group_of, *pieces, after=after)


def chosen(table, arrived, *after, flops=0):
    def body(t, s, *rest):
        for j in range(TPS):
            rest[-1][j] = s[t[j]]

    return copier(body, struct(*PIECES), table, arrived, after=after, flops=flops)


def outgoing_sums(owner, own, other):
    def body(t, a, b, *rest):
        for j in range(TPS):
            rest[-1][t[j]] = (a[j] + b[j].astype(F32)).astype(BF)

    return copier(body, struct(16, *PIECES[1:]), owner, own, other)


def chosen_pieces(group_of, arrived):
    def body(t, s, *outs):
        for j in range(TPS):
            for k in range(CHIPS):
                outs[k][j] = s[t[j], k]

    return copier(body, (struct(*PIECE),) * CHIPS, group_of, arrived)


def stored_tiles(peers, keys, values):
    def body(t, *rest):
        for part in range(2):
            for k in range(CHIPS):
                where = column(t[k] + part * KVH, HD)
                rest[-1][:, :, where] = rest[part * CHIPS + k][...]

    return copier(body, struct(TPS, ROWS, 2 * KW), peers, *keys, *values)


def text_rows(peers, chunks):
    def body(t, *rest):
        for k in range(CHIPS):
            rest[CHIPS][:, column(t[k], QW)] = rest[k][...]

    return copier(body, struct(TOK, HQ * HD), peers, *chunks)


LANES = [slice(i * HD, (i + 1) * HD) for i in range(TT // HD)]
HEADS = [slice(h * TOK, (h + 1) * TOK) for h in range(GROUP)]
CH_S, CH_O, CH_D = 256, 512, 512


def cuts(size):
    return [slice(i, i + size) for i in range(0, LINES, size)]


def wide(column, rows):
    return jnp.broadcast_to(column, (rows, HD))


def fill_tiles(core, target, mine, other):
    for k in range(CHIPS):
        here = pl.multiple_of(core * (TT // 2) + k * ROWS, 16)
        there = pl.multiple_of((1 - core) * (TT // 2) + k * ROWS, 16)

        @pl.loop(0, TPS)
        def _(j):
            target[j, pl.ds(here, ROWS), :] = mine[j, k]
            target[j, pl.ds(there, ROWS), :] = other[j, k]


def split_tiles(core, total, scale, mine, other):
    @pl.loop(0, TPS)
    def _(j):
        rows = (total[j] * scale).T
        halves = [rows[: TT // 2].reshape(CHIPS, ROWS, HD), rows[TT // 2 :].reshape(CHIPS, ROWS, HD)]
        for p in range(2):

            @pl.when(core == p)
            def _():
                mine[j] = halves[p]
                other[j] = halves[1 - p].astype(BF)


def load_text(b, target, chunks):
    for k, chunk in enumerate(chunks):

        @pl.when(b == k)
        def _():
            for h, rows in enumerate(HEADS):
                target[rows, :] = chunk[:, h * HD : (h + 1) * HD]


def store_text(b, chunks, value):
    for k, chunk in enumerate(chunks):

        @pl.when(b == k)
        def _():
            for h, rows in enumerate(HEADS):
                chunk[:, h * HD : (h + 1) * HD] = value(rows)


def weights_body(
    info, q0, q1, q2, q3, k_mine, k_other, e_out, w_out, k_s, kt_s, q_s, m_s, l_s, top_s, sum_s
):
    b = pl.program_id(0)
    first, number = info[0, b], info[1, b]

    @pl.when(b == 0)
    def _():
        fill_tiles(info[2, 1], k_s, k_mine, k_other)

        @pl.loop(0, TPS)
        def _(j):
            kt_s[j] = k_s[j].T

    load_text(b, q_s, (q0, q1, q2, q3))
    top_s[...] = jnp.full(top_s.shape, -jnp.inf, F32)
    sum_s[...] = jnp.zeros_like(sum_s)
    w_out[...] = jnp.zeros_like(w_out)

    @pl.loop(0, number)
    def _(t):
        j = first + t
        for rows in cuts(CH_S):
            s = jnp.dot(q_s[rows, :], kt_s[j], preferred_element_type=F32)
            top = s[:, LANES[0]]
            for part in LANES[1:]:
                top = jnp.maximum(top, s[:, part])
            top = wide(jnp.max(top, axis=1, keepdims=True), CH_S)
            m_s[t, rows, :] = top
            top_s[rows, :] = jnp.maximum(top_s[rows, :], top)
            top = top * EXP_SCALE
            total = None
            for part in LANES:
                e = jnp.exp2(s[:, part] * EXP_SCALE - top)
                e_out[0, t, rows, part] = e.astype(BF)
                total = e if total is None else total + e
            l_s[t, rows, :] = total

    @pl.loop(0, number)
    def _(t):
        f = jnp.exp2((m_s[t] - top_s[...]) * EXP_SCALE)
        m_s[t] = f
        sum_s[...] += f * l_s[t]

    for rows in HEADS:
        total = jnp.sum(sum_s[rows, :], axis=1, keepdims=True)
        sum_s[rows, :] = wide(1.0 / total, TOK)

    @pl.loop(0, number)
    def _(t):
        lane = lax.broadcasted_iota(jnp.int32, W_SHAPE, 1)
        w_out[0] = jnp.where(lane == t, m_s[t] * sum_s[...], w_out[0])


def outputs_body(
    info, g0, g1, g2, g3, e, w, v_mine, v_other, o0, o1, o2, o3, d_out, mine, other,
    v_s, dvt_s, d_s, acc_s,
):
    b = pl.program_id(0)
    core = info[2, 1]
    first, number = info[0, b], info[1, b]

    @pl.when(b == 0)
    def _():
        fill_tiles(core, v_s, v_mine, v_other)

        @pl.loop(0, TPS)
        def _(j):
            dvt_s[j] = jnp.zeros((HD, TT), F32)

    load_text(b, d_s, (g0, g1, g2, g3))
    acc_s[...] = jnp.zeros_like(acc_s)

    @pl.loop(0, number)
    def _(t):
        j = first + t
        lane = lax.broadcasted_iota(jnp.int32, (CH_O, HD), 1)
        for rows in cuts(CH_O):
            weight = jnp.sum(jnp.where(lane == t, w[0, rows, :], 0.0), axis=1, keepdims=True)
            acc_s[rows, :] += weight * jnp.dot(e[0, t, rows, :], v_s[j], preferred_element_type=F32)
            d_out[0, t, rows, :] = (d_s[rows, :].astype(F32) * weight).astype(BF)
        dvt_s[j] += jnp.dot(d_out[0, t].T, e[0, t], preferred_element_type=F32)

    store_text(b, (o0, o1, o2, o3), lambda rows: acc_s[rows, :].astype(BF))

    @pl.when(b == CHIPS - 1)
    def _():
        split_tiles(core, dvt_s, 1.0, mine, other)


def grads_body(
    info, q0, q1, q2, q3, e, d, a0, a1, a2, a3, k_mine, k_other, v_mine, v_other,
    o0, o1, o2, o3, mine, other,
    k_s, vt_s, dkt_s, q_s, acc_s, a_s, ds_s,
):
    b = pl.program_id(0)
    core = info[2, 1]
    first, number = info[0, b], info[1, b]

    @pl.when(b == 0)
    def _():
        fill_tiles(core, k_s, v_mine, v_other)

        @pl.loop(0, TPS)
        def _(j):
            vt_s[j] = k_s[j].T
            dkt_s[j] = jnp.zeros((HD, TT), F32)

        fill_tiles(core, k_s, k_mine, k_other)

    load_text(b, q_s, (q0, q1, q2, q3))
    load_text(b, a_s, (a0, a1, a2, a3))
    acc_s[...] = jnp.zeros_like(acc_s)

    @pl.loop(0, number)
    def _(t):
        j = first + t
        for rows in cuts(CH_D):
            dp = jnp.dot(d[0, t, rows, :], vt_s[j], preferred_element_type=F32)
            dot = jnp.sum(
                d[0, t, rows, :].astype(F32) * a_s[rows, :].astype(F32), axis=1, keepdims=True
            )
            ds = (e[0, t, rows, :].astype(F32) * (dp - dot)).astype(BF)
            ds_s[rows, :] = ds
            acc_s[rows, :] += jnp.dot(ds, k_s[j], preferred_element_type=F32)
        dkt_s[j] += jnp.dot(q_s[...].T, ds_s[...], preferred_element_type=F32)

    store_text(b, (o0, o1, o2, o3), lambda rows: (acc_s[rows, :] * SCALE).astype(BF))

    @pl.when(b == CHIPS - 1)
    def _():
        split_tiles(core, dkt_s, SCALE, mine, other)


def fixed(shape):
    zeros = (0,) * len(shape)
    return pl.BlockSpec(shape, lambda b, t: zeros, pipeline_mode=pl.Buffered(1))


def kept(shape):
    zeros = (0,) * len(shape)
    return pl.BlockSpec(shape, lambda b, t: zeros)


def by_block(*shape):
    zeros = (0,) * len(shape)
    return pl.BlockSpec((1,) + shape, lambda b, t: (b,) + zeros)


OWN_TEXT = pl.BlockSpec((TOK, QW), lambda b, t: (0, t[2, 0]), pipeline_mode=pl.Buffered(1))
E_SHAPE = (MAXT, LINES, TT)
D_SHAPE = (MAXT, LINES, HD)
W_SHAPE = (LINES, HD)


def attention_call(body, work, out_shape, in_specs, out_specs, scratch_shapes):
    return pl.pallas_call(
        body,
        out_shape=out_shape,
        grid_spec=pltpu.PrefetchScalarGridSpec(
            num_scalar_prefetch=1,
            grid=(CHIPS,),
            in_specs=in_specs,
            out_specs=out_specs,
            scratch_shapes=scratch_shapes,
        ),
        compiler_params=pltpu.CompilerParams(vmem_limit_bytes=56 * 2**20),
        cost_estimate=pl.CostEstimate(
            flops=work * 10**9,
            bytes_accessed=work * 2**20,
            transcendentals=0,
        ),
    )


TEXT = [OWN_TEXT] + [fixed((TOK, QW))] * 3
TEXT_OUT = (struct(TOK, QW),) * 4
TEXT_KEPT = (kept((TOK, QW)),) * 4
TILES = [fixed(PIECES)] * 2
TILES_OUT = (jax.ShapeDtypeStruct(PIECES, F32), struct(*PIECES))
TILES_KEPT = (kept(PIECES),) * 2
TILE_ROWS, TILE_COLUMNS = (TPS, TT, HD), (TPS, HD, TT)


def weights(info, queries, tiles):
    return attention_call(
        weights_body,
        0,
        (struct(CHIPS, *E_SHAPE), jax.ShapeDtypeStruct((CHIPS,) + W_SHAPE, F32)),
        TEXT + TILES,
        (by_block(*E_SHAPE), by_block(*W_SHAPE)),
        [
            pltpu.VMEM(TILE_ROWS, BF),
            pltpu.VMEM(TILE_COLUMNS, BF),
            pltpu.VMEM((LINES, HD), BF),
            pltpu.VMEM((MAXT, LINES, HD), F32),
            pltpu.VMEM((MAXT, LINES, HD), F32),
            pltpu.VMEM((LINES, HD), F32),
            pltpu.VMEM((LINES, HD), F32),
        ],
    )(info, *queries, *tiles)


def outputs(info, grads, e, w, tiles):
    return attention_call(
        outputs_body,
        40,
        TEXT_OUT + (struct(CHIPS, *D_SHAPE),) + TILES_OUT,
        TEXT + [by_block(*E_SHAPE), by_block(*W_SHAPE)] + TILES,
        TEXT_KEPT + (by_block(*D_SHAPE),) + TILES_KEPT,
        [
            pltpu.VMEM(TILE_ROWS, BF),
            pltpu.VMEM(TILE_COLUMNS, F32),
            pltpu.VMEM((LINES, HD), BF),
            pltpu.VMEM((LINES, HD), F32),
        ],
    )(info, *grads, e, w, *tiles)


def gradients(info, queries, e, d, attn, keys, values):
    return attention_call(
        grads_body,
        60,
        TEXT_OUT + TILES_OUT,
        TEXT
        + [by_block(*E_SHAPE), by_block(*D_SHAPE)]
        + [fixed((TOK, QW))] * 4
        + TILES * 2,
        TEXT_KEPT + TILES_KEPT,
        [
            pltpu.VMEM(TILE_ROWS, BF),
            pltpu.VMEM(TILE_COLUMNS, BF),
            pltpu.VMEM(TILE_COLUMNS, F32),
            pltpu.VMEM((LINES, HD), BF),
            pltpu.VMEM((LINES, HD), F32),
            pltpu.VMEM((LINES, HD), BF),
            pltpu.VMEM((LINES, TT), BF),
        ],
    )(info, *queries, e, d, *attn, *keys, *values)


def swap(x, mask):
    return lax.ppermute(x, "seq", [(i, i ^ mask) for i in range(N_SEQ)])


def spread(chunks):
    return [chunks[0]] + [swap(chunks[k], 2 * k) for k in range(1, CHIPS)]


def shards(queries, grad_out, kv_store, tile_owner, tile_counts, span_image):
    my_group = lax.axis_index("dp")
    my_seq = lax.axis_index("seq")
    chip, core = my_seq // 2, my_seq % 2
    queries, grad_out, store = queries[0], grad_out[0], kv_store[0]

    groups = jnp.arange(tile_owner.shape[0], dtype=jnp.int32)
    group_of = jnp.sum(jnp.where(tile_owner == my_group, groups[:, None], 0), axis=0).astype(
        jnp.int32
    )
    owner = lax.dynamic_index_in_dim(tile_owner, my_group, 0, keepdims=False)
    peers = (chip ^ jnp.arange(CHIPS, dtype=jnp.int32)).astype(jnp.int32)
    counts = lax.dynamic_index_in_dim(tile_counts, my_group, 0, keepdims=False)
    starts = jnp.cumsum(counts) - counts
    images = lax.dynamic_index_in_dim(span_image, my_group, 0, keepdims=False)
    blocks = peers * 2 + core
    mine = jnp.sum(
        jnp.where(blocks[:, None] == jnp.arange(N_SEQ)[None, :], images[None, :], 0), axis=1
    )
    pick = mine[:, None] == jnp.arange(IMGS, dtype=jnp.int32)[None, :]
    first = jnp.sum(jnp.where(pick, starts[None, :], 0), axis=1)
    number = jnp.sum(jnp.where(pick, counts[None, :], 0), axis=1)
    place = jnp.stack([chip, core, chip, core])
    info = jnp.stack([first, number, place]).astype(jnp.int32)

    def exchange(x):
        return lax.all_to_all(x, "dp", split_axis=0, concat_axis=0, tiled=True)

    k_pieces = outgoing_heads(peers, store, 0)
    pieces = outgoing_heads(peers, store, 1, queries, grad_out)
    v_pieces, texts = pieces[:CHIPS], pieces[CHIPS:]
    q_text = spread([queries, *texts[:3]])
    g_text = spread([grad_out, *texts[3:]])
    keys = exchange(outgoing_pieces(group_of, spread(k_pieces), v_pieces[0]))
    values = outgoing_pieces(group_of, spread(v_pieces), info)
    keys = chosen(owner, keys, values, *q_text[1:], flops=LONG)
    keys = keys, swap(keys, 1)
    e, w = weights(info, q_text, keys)
    values = chosen(owner, exchange(values), e, *g_text[1:])
    values = values, swap(values, 1)

    *attn, d, dv_mine, dv_other = outputs(info, g_text, e, w, values)
    attn_text = spread(attn)
    *grad_q, dk_mine, dk_other = gradients(info, q_text, e, d, attn, keys, values)
    dk_other = fence(dk_other, *attn_text[1:])

    def scatter(own, other):
        arrived = exchange(outgoing_sums(owner, own, swap(other, 1)))
        return spread(chosen_pieces(group_of, arrived))

    dv = scatter(dv_mine, dv_other)
    dk = scatter(dk_mine, dk_other)
    grad_kv = stored_tiles(peers, dk, dv)
    attn_rows = text_rows(peers, attn_text)
    grad_rows = text_rows(peers, spread(grad_q))
    return (attn_rows[None], grad_rows[None], grad_kv[None])


def solution(mesh):
    placed = (P("dp", "seq", None), P("dp", "seq", None), P("dp", None, "seq", None), P(), P(), P())
    return jax.shard_map(
        shards,
        mesh=mesh,
        in_specs=placed,
        out_specs=(P("dp", "seq", None), P("dp", "seq", None), P("dp", None, "seq", None)),
        check_vma=False,
    )
```

```python
import jax
import jax.numpy as jnp
from jax import lax
from jax.experimental import pallas as pl
from jax.experimental.pallas import tpu as pltpu
from jax.sharding import PartitionSpec as P

HD = 128
HQ = 32
KVH = 4
GROUP = 8
TT = 640
TPS = 8
IMGS = 3
MAXT = 4
TOK = 128
N_SEQ = 8
CHIPS = 4
ROWS = TT // N_SEQ
KW = KVH * HD
QW = GROUP * HD
LINES = GROUP * TOK
SCALE = HD**-0.5
PIECE = (TPS, ROWS, HD)
PIECES = (TPS, CHIPS, ROWS, HD)
EXP_SCALE = SCALE * 1.4426950408889634
LONG = 10**11
BF = jnp.bfloat16
F32 = jnp.float32


def run_copies(pairs):
    for (source, where), (target, there) in pairs:
        target[there] = source[where]


def whole(shape):
    zeros = (0,) * len(shape)
    return pl.BlockSpec(shape, lambda i, t: zeros)


def copier(body, shapes, table, *arrays, after=(), flops=0):
    return pl.pallas_call(
        body,
        out_shape=shapes,
        grid_spec=pltpu.PrefetchScalarGridSpec(
            num_scalar_prefetch=1,
            grid=(1,),
            in_specs=[whole(a.shape) for a in arrays]
            + [pl.BlockSpec(memory_space=pl.ANY)] * len(after),
            out_specs=jax.tree.map(lambda a: whole(a.shape), shapes),
        ),
        compiler_params=pltpu.CompilerParams(vmem_limit_bytes=32 * 2**20),
        cost_estimate=pl.CostEstimate(flops=flops, bytes_accessed=2**22, transcendentals=0),
    )(table, *arrays, *after)


def struct(*shape):
    return jax.ShapeDtypeStruct(shape, BF)


def column(index, width):
    return pl.ds(pl.multiple_of(index * width, width), width)


def outgoing_heads(peers, store, part, *text):
    def body(t, s, *rest):
        outs = rest[len(text) :]
        for k in range(CHIPS):
            outs[k][...] = s[:, :, column(t[k], HD)]
        for i in range(len(text)):
            for k in range(1, CHIPS):
                outs[CHIPS + 3 * i + k - 1][...] = rest[i][:, column(t[k], QW)]

    shapes = (struct(*PIECE),) * CHIPS + (struct(TOK, QW),) * (3 * len(text))
    return pl.pallas_call(
        body,
        out_shape=shapes,
        grid_spec=pltpu.PrefetchScalarGridSpec(
            num_scalar_prefetch=1,
            grid=(1,),
            in_specs=[pl.BlockSpec((TPS, ROWS, KW), lambda i, t: (0, 0, part))]
            + [whole(x.shape) for x in text],
            out_specs=jax.tree.map(lambda a: whole(a.shape), shapes),
        ),
        compiler_params=pltpu.CompilerParams(vmem_limit_bytes=32 * 2**20),
    )(peers, store, *text)


def fence(x, *after):
    def body(*refs):
        pass

    return pl.pallas_call(
        body,
        out_shape=jax.ShapeDtypeStruct(x.shape, x.dtype),
        in_specs=[pl.BlockSpec(memory_space=pl.ANY)] * (1 + len(after)),
        out_specs=pl.BlockSpec(memory_space=pl.ANY),
        input_output_aliases={0: 0},
    )(x, *after)


def outgoing_pieces(group_of, pieces, *after):
    def body(t, *rest):
        for j in range(TPS):
            for k in range(CHIPS):
                rest[-1][t[j], k] = rest[k][j]

    return copier(body, struct(16, *PIECES[1:]), group_of, *pieces, after=after)


def chosen(table, arrived, *after, flops=0):
    def body(t, s, *rest):
        for j in range(TPS):
            rest[-1][j] = s[t[j]]

    return copier(body, struct(*PIECES), table, arrived, after=after, flops=flops)


def outgoing_sums(owner, own, other):
    def body(t, a, b, *rest):
        for j in range(TPS):
            rest[-1][t[j]] = (a[j].astype(F32) + b[j].astype(F32)).astype(BF)

    return copier(body, struct(16, *PIECES[1:]), owner, own, other)


def chosen_pieces(group_of, arrived):
    def body(t, s, *outs):
        for j in range(TPS):
            for k in range(CHIPS):
                outs[k][j] = s[t[j], k]

    return copier(body, (struct(*PIECE),) * CHIPS, group_of, arrived)


def stored_tiles(peers, keys, values):
    def body(t, *rest):
        for part in range(2):
            for k in range(CHIPS):
                where = column(t[k] + part * KVH, HD)
                rest[-1][:, :, where] = rest[part * CHIPS + k][...]

    return copier(body, struct(TPS, ROWS, 2 * KW), peers, *keys, *values)


def text_rows(peers, chunks):
    def body(t, *rest):
        for k in range(CHIPS):
            rest[CHIPS][:, column(t[k], QW)] = rest[k][...]

    return copier(body, struct(TOK, HQ * HD), peers, *chunks)


LANES = [slice(i * HD, (i + 1) * HD) for i in range(TT // HD)]
HEADS = [slice(h * TOK, (h + 1) * TOK) for h in range(GROUP)]
CH_S, CH_O, CH_D = 128, 512, 512


def cuts(size):
    return [slice(i, i + size) for i in range(0, LINES, size)]


def wide(column, rows):
    return jnp.broadcast_to(column, (rows, HD))


def fill_tiles(core, target, mine, other):
    for k in range(CHIPS):
        here = pl.multiple_of(core * (TT // 2) + k * ROWS, 16)
        there = pl.multiple_of((1 - core) * (TT // 2) + k * ROWS, 16)

        @pl.loop(0, TPS)
        def _(j):
            target[j, pl.ds(here, ROWS), :] = mine[j, k]
            target[j, pl.ds(there, ROWS), :] = other[j, k]


def split_tiles(core, total, scale, mine, other):
    @pl.loop(0, TPS)
    def _(j):
        rows = (total[j] * scale).T
        halves = [rows[: TT // 2].reshape(CHIPS, ROWS, HD), rows[TT // 2 :].reshape(CHIPS, ROWS, HD)]
        for p in range(2):

            @pl.when(core == p)
            def _():
                mine[j] = halves[p].astype(BF)
                other[j] = halves[1 - p].astype(BF)


def load_text(b, target, chunks):
    for k, chunk in enumerate(chunks):

        @pl.when(b == k)
        def _():
            for h, rows in enumerate(HEADS):
                target[rows, :] = chunk[:, h * HD : (h + 1) * HD]


def store_text(b, chunks, value):
    for k, chunk in enumerate(chunks):

        @pl.when(b == k)
        def _():
            for h, rows in enumerate(HEADS):
                chunk[:, h * HD : (h + 1) * HD] = value(rows)


def weights_body(
    info, q0, q1, q2, q3, k_mine, k_other, e_out, w_out, k_s, kt_s, q_s, m_s, l_s, top_s, sum_s
):
    b = pl.program_id(0)
    first, number = info[0, b], info[1, b]

    @pl.when(b == 0)
    def _():
        fill_tiles(info[2, 1], k_s, k_mine, k_other)

        @pl.loop(0, TPS)
        def _(j):
            kt_s[j] = k_s[j].T

    load_text(b, q_s, (q0, q1, q2, q3))
    top_s[...] = jnp.full(top_s.shape, -jnp.inf, F32)
    sum_s[...] = jnp.zeros_like(sum_s)
    w_out[...] = jnp.zeros_like(w_out)

    @pl.loop(0, number)
    def _(t):
        j = first + t
        for rows in cuts(CH_S):
            s = jnp.dot(q_s[rows, :], kt_s[j], preferred_element_type=F32)
            top = s[:, LANES[0]]
            for part in LANES[1:]:
                top = jnp.maximum(top, s[:, part])
            top = wide(jnp.max(top, axis=1, keepdims=True), CH_S)
            m_s[t, rows, :] = top
            top_s[rows, :] = jnp.maximum(top_s[rows, :], top)
            top = top * EXP_SCALE
            total = None
            for part in LANES:
                e = jnp.exp2(s[:, part] * EXP_SCALE - top)
                e_out[0, t, rows, part] = e.astype(BF)
                total = e if total is None else total + e
            l_s[t, rows, :] = total

    @pl.loop(0, number)
    def _(t):
        f = jnp.exp2((m_s[t] - top_s[...]) * EXP_SCALE)
        m_s[t] = f
        sum_s[...] += f * l_s[t]

    for rows in HEADS:
        total = jnp.sum(sum_s[rows, :], axis=1, keepdims=True)
        sum_s[rows, :] = wide(1.0 / total, TOK)

    @pl.loop(0, number)
    def _(t):
        lane = lax.broadcasted_iota(jnp.int32, W_SHAPE, 1)
        w_out[0] = jnp.where(lane == t, m_s[t] * sum_s[...], w_out[0])


def outputs_body(
    info, g0, g1, g2, g3, e, w, v_mine, v_other, o0, o1, o2, o3, d_out, mine, other,
    v_s, dvt_s, d_s, acc_s,
):
    b = pl.program_id(0)
    core = info[2, 1]
    first, number = info[0, b], info[1, b]

    @pl.when(b == 0)
    def _():
        fill_tiles(core, v_s, v_mine, v_other)

        @pl.loop(0, TPS)
        def _(j):
            dvt_s[j] = jnp.zeros((HD, TT), F32)

    load_text(b, d_s, (g0, g1, g2, g3))
    acc_s[...] = jnp.zeros_like(acc_s)

    @pl.loop(0, number)
    def _(t):
        j = first + t
        lane = lax.broadcasted_iota(jnp.int32, (CH_O, HD), 1)
        for rows in cuts(CH_O):
            weight = jnp.sum(jnp.where(lane == t, w[0, rows, :], 0.0), axis=1, keepdims=True)
            acc_s[rows, :] += weight * jnp.dot(e[0, t, rows, :], v_s[j], preferred_element_type=F32)
            d_out[0, t, rows, :] = (d_s[rows, :].astype(F32) * weight).astype(BF)
        dvt_s[j] += jnp.dot(d_out[0, t].T, e[0, t], preferred_element_type=F32)

    store_text(b, (o0, o1, o2, o3), lambda rows: acc_s[rows, :].astype(BF))

    @pl.when(b == CHIPS - 1)
    def _():
        split_tiles(core, dvt_s, 1.0, mine, other)


def grads_body(
    info, q0, q1, q2, q3, e, d, a0, a1, a2, a3, k_mine, k_other, v_mine, v_other,
    o0, o1, o2, o3, mine, other,
    k_s, vt_s, dkt_s, q_s, acc_s, a_s, ds_s,
):
    b = pl.program_id(0)
    core = info[2, 1]
    first, number = info[0, b], info[1, b]

    @pl.when(b == 0)
    def _():
        fill_tiles(core, k_s, v_mine, v_other)

        @pl.loop(0, TPS)
        def _(j):
            vt_s[j] = k_s[j].T
            dkt_s[j] = jnp.zeros((HD, TT), F32)

        fill_tiles(core, k_s, k_mine, k_other)

    load_text(b, q_s, (q0, q1, q2, q3))
    load_text(b, a_s, (a0, a1, a2, a3))
    acc_s[...] = jnp.zeros_like(acc_s)

    @pl.loop(0, number)
    def _(t):
        j = first + t
        for rows in cuts(CH_D):
            dp = jnp.dot(d[0, t, rows, :], vt_s[j], preferred_element_type=F32)
            dot = jnp.sum(
                d[0, t, rows, :].astype(F32) * a_s[rows, :].astype(F32), axis=1, keepdims=True
            )
            ds = (e[0, t, rows, :].astype(F32) * (dp - dot)).astype(BF)
            ds_s[rows, :] = ds
            acc_s[rows, :] += jnp.dot(ds, k_s[j], preferred_element_type=F32)
        dkt_s[j] += jnp.dot(q_s[...].T, ds_s[...], preferred_element_type=F32)

    store_text(b, (o0, o1, o2, o3), lambda rows: (acc_s[rows, :] * SCALE).astype(BF))

    @pl.when(b == CHIPS - 1)
    def _():
        split_tiles(core, dkt_s, SCALE, mine, other)


def fixed(shape):
    zeros = (0,) * len(shape)
    return pl.BlockSpec(shape, lambda b, t: zeros, pipeline_mode=pl.Buffered(1))


def kept(shape):
    zeros = (0,) * len(shape)
    return pl.BlockSpec(shape, lambda b, t: zeros)


def by_block(*shape):
    zeros = (0,) * len(shape)
    return pl.BlockSpec((1,) + shape, lambda b, t: (b,) + zeros)


OWN_TEXT = pl.BlockSpec((TOK, QW), lambda b, t: (0, t[2, 0]), pipeline_mode=pl.Buffered(1))
E_SHAPE = (MAXT, LINES, TT)
D_SHAPE = (MAXT, LINES, HD)
W_SHAPE = (LINES, HD)


def attention_call(body, work, out_shape, in_specs, out_specs, scratch_shapes):
    return pl.pallas_call(
        body,
        out_shape=out_shape,
        grid_spec=pltpu.PrefetchScalarGridSpec(
            num_scalar_prefetch=1,
            grid=(CHIPS,),
            in_specs=in_specs,
            out_specs=out_specs,
            scratch_shapes=scratch_shapes,
        ),
        compiler_params=pltpu.CompilerParams(vmem_limit_bytes=56 * 2**20),
        cost_estimate=pl.CostEstimate(
            flops=work * 10**9,
            bytes_accessed=work * 2**20,
            transcendentals=0,
        ),
    )


TEXT = [OWN_TEXT] + [fixed((TOK, QW))] * 3
TEXT_OUT = (struct(TOK, QW),) * 4
TEXT_KEPT = (kept((TOK, QW)),) * 4
TILES = [fixed(PIECES)] * 2
TILES_OUT = (struct(*PIECES),) * 2
TILES_KEPT = (kept(PIECES),) * 2
TILE_ROWS, TILE_COLUMNS = (TPS, TT, HD), (TPS, HD, TT)


def weights(info, queries, tiles):
    return attention_call(
        weights_body,
        0,
        (struct(CHIPS, *E_SHAPE), jax.ShapeDtypeStruct((CHIPS,) + W_SHAPE, F32)),
        TEXT + TILES,
        (by_block(*E_SHAPE), by_block(*W_SHAPE)),
        [
            pltpu.VMEM(TILE_ROWS, BF),
            pltpu.VMEM(TILE_COLUMNS, BF),
            pltpu.VMEM((LINES, HD), BF),
            pltpu.VMEM((MAXT, LINES, HD), F32),
            pltpu.VMEM((MAXT, LINES, HD), F32),
            pltpu.VMEM((LINES, HD), F32),
            pltpu.VMEM((LINES, HD), F32),
        ],
    )(info, *queries, *tiles)


def outputs(info, grads, e, w, tiles):
    return attention_call(
        outputs_body,
        40,
        TEXT_OUT + (struct(CHIPS, *D_SHAPE),) + TILES_OUT,
        TEXT + [by_block(*E_SHAPE), by_block(*W_SHAPE)] + TILES,
        TEXT_KEPT + (by_block(*D_SHAPE),) + TILES_KEPT,
        [
            pltpu.VMEM(TILE_ROWS, BF),
            pltpu.VMEM(TILE_COLUMNS, F32),
            pltpu.VMEM((LINES, HD), BF),
            pltpu.VMEM((LINES, HD), F32),
        ],
    )(info, *grads, e, w, *tiles)


def gradients(info, queries, e, d, attn, keys, values):
    return attention_call(
        grads_body,
        60,
        TEXT_OUT + TILES_OUT,
        TEXT
        + [by_block(*E_SHAPE), by_block(*D_SHAPE)]
        + [fixed((TOK, QW))] * 4
        + TILES * 2,
        TEXT_KEPT + TILES_KEPT,
        [
            pltpu.VMEM(TILE_ROWS, BF),
            pltpu.VMEM(TILE_COLUMNS, BF),
            pltpu.VMEM(TILE_COLUMNS, F32),
            pltpu.VMEM((LINES, HD), BF),
            pltpu.VMEM((LINES, HD), F32),
            pltpu.VMEM((LINES, HD), BF),
            pltpu.VMEM((LINES, TT), BF),
        ],
    )(info, *queries, e, d, *attn, *keys, *values)


def swap(x, mask):
    return lax.ppermute(x, "seq", [(i, i ^ mask) for i in range(N_SEQ)])


def spread(chunks):
    return [chunks[0]] + [swap(chunks[k], 2 * k) for k in range(1, CHIPS)]


def shards(queries, grad_out, kv_store, tile_owner, tile_counts, span_image):
    my_group = lax.axis_index("dp")
    my_seq = lax.axis_index("seq")
    chip, core = my_seq // 2, my_seq % 2
    queries, grad_out, store = queries[0], grad_out[0], kv_store[0]

    groups = jnp.arange(tile_owner.shape[0], dtype=jnp.int32)
    group_of = jnp.sum(jnp.where(tile_owner == my_group, groups[:, None], 0), axis=0).astype(
        jnp.int32
    )
    owner = lax.dynamic_index_in_dim(tile_owner, my_group, 0, keepdims=False)
    peers = (chip ^ jnp.arange(CHIPS, dtype=jnp.int32)).astype(jnp.int32)
    counts = lax.dynamic_index_in_dim(tile_counts, my_group, 0, keepdims=False)
    starts = jnp.cumsum(counts) - counts
    images = lax.dynamic_index_in_dim(span_image, my_group, 0, keepdims=False)
    blocks = peers * 2 + core
    mine = jnp.sum(
        jnp.where(blocks[:, None] == jnp.arange(N_SEQ)[None, :], images[None, :], 0), axis=1
    )
    pick = mine[:, None] == jnp.arange(IMGS, dtype=jnp.int32)[None, :]
    first = jnp.sum(jnp.where(pick, starts[None, :], 0), axis=1)
    number = jnp.sum(jnp.where(pick, counts[None, :], 0), axis=1)
    place = jnp.stack([chip, core, chip, core])
    info = jnp.stack([first, number, place]).astype(jnp.int32)

    def exchange(x):
        return lax.all_to_all(x, "dp", split_axis=0, concat_axis=0, tiled=True)

    k_pieces = outgoing_heads(peers, store, 0)
    pieces = outgoing_heads(peers, store, 1, queries, grad_out)
    v_pieces, texts = pieces[:CHIPS], pieces[CHIPS:]
    q_text = spread([queries, *texts[:3]])
    g_text = spread([grad_out, *texts[3:]])
    keys = exchange(outgoing_pieces(group_of, spread(k_pieces), v_pieces[0]))
    values = outgoing_pieces(group_of, spread(v_pieces), info)
    keys = chosen(owner, keys, values, *q_text[1:], flops=LONG)
    keys = keys, swap(keys, 1)
    e, w = weights(info, q_text, keys)
    values = chosen(owner, exchange(values), e, *g_text[1:])
    values = values, swap(values, 1)

    *attn, d, dv_mine, dv_other = outputs(info, g_text, e, w, values)
    attn_text = spread(attn)
    *grad_q, dk_mine, dk_other = gradients(info, q_text, e, d, attn, keys, values)
    dk_other = fence(dk_other, *attn_text[1:])

    def scatter(own, other):
        arrived = exchange(outgoing_sums(owner, own, swap(other, 1)))
        return spread(chosen_pieces(group_of, arrived))

    dv = scatter(dv_mine, dv_other)
    dk = scatter(dk_mine, dk_other)
    grad_kv = stored_tiles(peers, dk, dv)
    attn_rows = text_rows(peers, attn_text)
    grad_rows = text_rows(peers, spread(grad_q))
    return (attn_rows[None], grad_rows[None], grad_kv[None])


def solution(mesh):
    placed = (P("dp", "seq", None), P("dp", "seq", None), P("dp", None, "seq", None), P(), P(), P())
    return jax.shard_map(
        shards,
        mesh=mesh,
        in_specs=placed,
        out_specs=(P("dp", "seq", None), P("dp", "seq", None), P("dp", None, "seq", None)),
        check_vma=False,
    )
```
